512 devices in a mesh: param: 16 (over y, x_lo, core), example: 32 (over z, x_hi).
Axes of the slice: x: 4 (x_hi: 2, x_lo: 2; x = x_hi * 2 + x_lo), y: 4, z: 16, core: 2. Of those that a mesh axis runs over, the one named last changes fastest.
Arguments:
- train_grads: bfloat16 [24576, 32768], P('example', 'param'), may hold values from -6 to 6
- query_cache: bfloat16 [32, 256, 32768], P('example', None, 'param'), may hold values from -6 to 6
- left_inverse: float32 [32, 32, 32], replicated
- right_inverse: float32 [32, 32, 32], replicated
- module_of: int32 [32], replicated, may hold values from 0 to 31, each once
- owner: int32 [4], replicated, may hold values from 0 to 31, as said below
Outputs:
- scores: float32 [256, 4, 24576], P('param', None, 'example')
The draws below stay inside these ranges and needn't reach their ends.
Inputs may be any that keep to these rules, and one draw needn't show every extreme that they name: A permutation: stored block j holds module module_of[j]. `owner`: the first and the last slot are each used in some turn.
All inputs are finite; a program needn't handle non-finite values.
Results may differ from the reference program's by a relative error of at most 0.0029.
Values may be sent and summed in bfloat16 or wider, within the bound.
A program may use at most 64 MiB of HBM per device.

```python
import math
import jax
import jax.numpy as jnp
from jax import lax

KIN = 32
KOUT = 32
QB = 256
TURNS = 4
MODULES = 32
COORDS = 32768
ROWS = 24576
QSLOTS = 32
N_PARAM = 16


def assemble(key, diagonal, size):
    noise = jax.random.normal(key, (diagonal.shape[0], size, size), jnp.float32)
    symmetric = (noise + jnp.swapaxes(noise, 1, 2)) * (0.156 / math.sqrt(size))
    return symmetric + diagonal[:, :, None] * jnp.eye(size, dtype=jnp.float32)[None, :, :]


def draw_left_inverse(key, part):
    key = jax.random.fold_in(key, 11)
    first, second = jax.random.split(key)
    diagonal = jnp.exp(jax.random.uniform(first, (MODULES, KIN), jnp.float32, math.log(0.5), math.log(2.0)))
    return assemble(second, diagonal, KIN)


def draw_right_inverse(key, part):
    key = jax.random.fold_in(key, 23)
    first, second = jax.random.split(key)
    diagonal = jnp.exp(jax.random.uniform(first, (MODULES, KOUT), jnp.float32, math.log(0.5), math.log(2.0)))
    return assemble(second, diagonal, KOUT)


def draw_owner(key, part):
    key = jax.random.fold_in(key, 37)
    first, second = jax.random.split(key)
    values = jax.random.randint(first, (TURNS,), 0, QSLOTS, dtype=jnp.int32)
    order = jax.random.permutation(second, TURNS)
    values = values.at[order[0]].set(0)
    values = values.at[order[1]].set(QSLOTS - 1)
    return values.astype(jnp.int32)


def block_levels(key, shape, cuts, least, high):
    def one(axis_at, shards_of):
        steps = jax.random.uniform(jax.random.fold_in(jax.random.fold_in(key, 6), axis_at), (shards_of,), jnp.float32, least / len(cuts), high / len(cuts))
        return jnp.repeat(jnp.exp(steps), shape[axis_at] // shards_of).reshape((-1,) + (1,) * (len(shape) - axis_at - 1))

    level = one(*cuts[0])
    for cut in cuts[1:]:
        level = level * one(*cut)
    return level


def gaussian(rng, dims, scale, limit, cuts=(), kind=jnp.bfloat16):
    level = block_levels(rng, dims, cuts, -0.22, 0.18) if cuts else 1.0
    drawn = jax.random.normal(rng, dims, jnp.float32) * scale * level
    return jnp.minimum(jnp.maximum(drawn, -limit), limit).astype(kind)


def setup_inputs(seed: int = 0) -> dict:
    streams_of = jax.random.split(jax.random.key(seed), 7)
    train_grads = gaussian(streams_of[0], (ROWS, COORDS), 1.0, 6.0, ((0, 32), (1, 16)))
    query_cache = gaussian(streams_of[1], (QSLOTS, QB, COORDS), 1.0, 6.0, ((0, 32), (2, 16)))
    left_inverse = draw_left_inverse(jax.random.fold_in(streams_of[6], 71), 0)
    right_inverse = draw_right_inverse(jax.random.fold_in(streams_of[6], 71), 0)
    module_of = jax.random.permutation(streams_of[4], MODULES).astype(jnp.int32)
    owner = draw_owner(jax.random.fold_in(streams_of[6], 71), 0)
    return {"train_grads": train_grads, "query_cache": query_cache, "left_inverse": left_inverse, "right_inverse": right_inverse, "module_of": module_of, "owner": owner}


def reference(train_grads, query_cache, left_inverse, right_inverse, module_of, owner):
    left_used = left_inverse[module_of]
    right_used = right_inverse[module_of]
    group = COORDS // N_PARAM
    factor = 1.0 / math.sqrt(COORDS)
    results = []
    for turn in range(TURNS):
        raw = lax.dynamic_index_in_dim(query_cache, owner[turn], 0, keepdims=False)
        blocks = raw.astype(jnp.float32).reshape(QB, MODULES, KIN, KOUT)
        mixed = jnp.einsum('mab,qmbc,mcd->qmad', left_used, blocks, right_used, precision=lax.Precision.HIGHEST)
        whitened = (mixed * factor).reshape(QB, COORDS).astype(jnp.bfloat16)

        def add_group(total, index):
            start = (index * group).astype(jnp.int32)
            query_piece = lax.dynamic_slice_in_dim(whitened, start, group, 1)
            train_piece = lax.dynamic_slice_in_dim(train_grads, start, group, 1)
            partial_value = jnp.dot(query_piece, train_piece.T, preferred_element_type=jnp.float32)
            return (total + partial_value, None)
        start_total = jnp.zeros((QB, ROWS), jnp.float32)
        total, unused = lax.scan(add_group, start_total, jnp.arange(N_PARAM, dtype=jnp.int32))
        results.append(total)
    return jnp.stack(results, axis=1)
```

```python
import functools
import math

import jax
import jax.numpy as jnp
from jax import lax
from jax.experimental import pallas as pl
from jax.experimental.pallas import tpu as pltpu
from jax.sharding import PartitionSpec as P

LANES = 256
DELAY = 3
MESH = pl.DeviceIdType.MESH


def kernel(
    cfg,
    train_hbm,
    query_hbm,
    left_ref,
    right_ref,
    module_ref,
    owner_ref,
    out_ref,
    query,
    train,
    spread_left,
    spread_right,
    kron_high,
    kron_low,
    mine,
    other,
    landed,
    passed,
    total,
    kept,
    outgoing,
    incoming,
    load_sem,
    swap_send,
    swap_recv,
    ring_send,
    ring_recv,
    sum_send,
    sum_recv,
):
    groups, ring, turns, rows, coords, steps, half, lanes, delay = cfg
    pieces = coords // lanes
    blocks = coords // 1024
    param = lax.axis_index("param")
    example = lax.axis_index("example")
    plane = lax.div(example, 2)
    side = lax.rem(example, 2)
    partner = plane * 2 + 1 - side
    following = lax.rem(plane + 1, ring) * 2 + side
    previous = lax.rem(plane + ring - 1, ring) * 2 + side
    lag = (ring - 1) * delay
    sent = steps - delay

    barrier = pltpu.get_barrier_semaphore()
    for place in (partner, following, previous):
        pl.semaphore_signal(
            barrier, inc=1, device_id={"example": place}, device_id_type=MESH
        )

    @pl.loop(1, groups)
    def _(hop):
        pl.semaphore_signal(
            barrier,
            inc=1,
            device_id={"param": lax.rem(param + hop, groups)},
            device_id_type=MESH,
        )

    load_query = pltpu.make_async_copy(query_hbm.at[0], query, load_sem.at[0])
    load_query.start()
    load_train = [
        pltpu.make_async_copy(
            train_hbm.at[:, pl.ds(k * lanes, lanes)], train.at[k], load_sem.at[1 + k]
        )
        for k in range(pieces)
    ]
    for copy in load_train:
        copy.start()

    factor = 1.0 / math.sqrt(coords * groups)
    col = lax.broadcasted_iota(jnp.int32, (32, 1024), 1)
    row = lax.broadcasted_iota(jnp.int32, (32, 1024), 0)
    pick_outer = (lax.shift_right_logical(col, 5) == row).astype(jnp.float32)
    pick_inner = (lax.bitwise_and(col, 31) == row).astype(jnp.float32)
    load_query.wait()
    for block in range(blocks):
        module = module_ref[param * blocks + block]
        spread_left[...] = lax.dot_general(
            left_ref[module] * factor,
            pick_outer,
            (((0,), (0,)), ((), ())),
            precision=lax.Precision.HIGHEST,
            preferred_element_type=jnp.float32,
        )
        spread_right[...] = lax.dot_general(
            right_ref[module],
            pick_inner,
            (((1,), (0,)), ((), ())),
            precision=lax.Precision.HIGHEST,
            preferred_element_type=jnp.float32,
        )

        @pl.loop(0, 32)
        def _(b):
            product = spread_left[pl.ds(b, 1), :] * spread_right[...]
            high = product.astype(jnp.bfloat16)
            low = (product - high.astype(jnp.float32)).astype(jnp.bfloat16)
            at = pl.ds(pl.multiple_of(b * 32, 32), 32)
            kron_high[at, :] = high
            kron_low[at, :] = low

        source = query[:, block * 1024 : (block + 1) * 1024]
        for k in range(1024 // lanes):
            cut = slice(k * lanes, (k + 1) * lanes)
            mixed = jnp.dot(
                source, kron_high[:, cut], preferred_element_type=jnp.float32
            ) + jnp.dot(source, kron_low[:, cut], preferred_element_type=jnp.float32)
            mine[:, block * (1024 // lanes) + k] = mixed.astype(jnp.bfloat16).reshape(
                groups, 16, lanes
            )

    pl.semaphore_wait(barrier, groups + 2)

    def place_of(order):
        return lax.rem(order + param, groups)

    def swap(order):
        at = place_of(order)
        return pltpu.make_async_remote_copy(
            src_ref=mine.at[at],
            dst_ref=other.at[at],
            send_sem=swap_send.at[order],
            recv_sem=swap_recv.at[order],
            device_id={"example": partner},
            device_id_type=MESH,
        )

    @pl.loop(0, groups // 2)
    def _(j):
        swap(j).start()
        swap(groups - 1 - j).start()

    roots = [lax.div(owner_ref[t], 2) for t in range(turns)]
    sides = [lax.rem(owner_ref[t], 2) for t in range(turns)]
    ahead = [lax.rem(plane - r + ring, ring) for r in roots]
    behind = [lax.rem(r - plane + ring, ring) for r in roots]

    def ring_copy(way, s):
        at = way * steps + s
        land = way * sent + s
        return pltpu.make_async_remote_copy(
            src_ref=passed.at[at],
            dst_ref=landed.at[land],
            send_sem=ring_send.at[land],
            recv_sem=ring_recv.at[land],
            device_id={"example": following if way == 0 else previous},
            device_id_type=MESH,
        )

    def advance(s, first, last):
        j = lax.div(s, pieces)
        k = lax.rem(s, pieces)

        @pl.when(jnp.logical_and(k == 0, j < groups // 2))
        def _():
            swap(j).wait_recv()
            swap(groups - 1 - j).wait_recv()

        for way in range(2):
            order = j if way == 0 else groups - 1 - j
            piece = k if way == 0 else pieces - 1 - k
            here = mine[place_of(order), piece]
            there = other[place_of(order), piece]
            if not first:
                ring_copy(way, s - delay).wait_recv()
            for t in range(turns):
                value = jnp.where(sides[t] == side, here, there)
                if not first:
                    value = jnp.where(
                        ahead[t] == 0, value, landed[way * sent + s - delay, t]
                    )
                passed[way * steps + s, t] = value
            if not last:
                ring_copy(way, s).start()

    def sum_copy(order):
        return pltpu.make_async_remote_copy(
            src_ref=outgoing.at[order],
            dst_ref=incoming.at[order],
            send_sem=sum_send.at[order],
            recv_sem=sum_recv.at[order],
            device_id={"param": place_of(order)},
            device_id_type=MESH,
        )

    def compute(i):
        j = lax.div(i, pieces)
        k = lax.rem(i, pieces)
        for way in range(2):
            near, far = (ahead, behind) if way == 0 else (behind, ahead)
            parts = []
            for t in range(turns):
                direct = i + delay * near[t]
                around = (2 * half - 1 - i) + delay * far[t]
                at = jnp.where(
                    direct < steps, way * steps + direct, (1 - way) * steps + around
                )
                parts.append(passed[at, t])
            left = jnp.concatenate(parts, axis=0)
            piece = k if way == 0 else pieces - 1 - k
            product = lax.dot_general(
                left,
                train[piece],
                (((1,), (1,)), ((), ())),
                preferred_element_type=jnp.float32,
            )

            @pl.when(k == 0)
            def _():
                total[way] = product

            @pl.when(k > 0)
            def _():
                total[way] += product

        @pl.when(k == pieces - 1)
        def _():
            @pl.when(j == 0)
            def _():
                kept[...] = total[0]

            @pl.when(j > 0)
            def _():
                outgoing[j] = total[0].astype(jnp.bfloat16)
                sum_copy(j).start()

            outgoing[groups - 1 - j] = total[1].astype(jnp.bfloat16)
            sum_copy(groups - 1 - j).start()

    @pl.loop(0, delay)
    def _(s):
        advance(s, True, False)

    @pl.loop(delay, lag)
    def _(s):
        advance(s, False, False)

    for copy in load_train:
        copy.wait()

    @pl.loop(lag, sent)
    def _(s):
        advance(s, False, False)
        compute(s - lag)

    @pl.loop(sent, steps)
    def _(s):
        advance(s, False, True)
        compute(s - lag)

    @pl.loop(steps - lag, half)
    def _(i):
        compute(i)

    @pl.loop(0, sent)
    def _(s):
        ring_copy(0, s).wait_send()
        ring_copy(1, s).wait_send()

    @pl.loop(0, groups)
    def _(order):
        swap(order).wait_send()

    @pl.loop(1, groups)
    def _(order):
        sum_copy(order).wait()
        kept[...] += incoming[order].astype(jnp.float32)

    for t in range(turns):
        out_ref[:, t, :] = kept[t * 16 : (t + 1) * 16, :]


def body(train_grads, query_cache, left_inverse, right_inverse, module_of, owner):
    groups = lax.axis_size("param")
    ring = lax.axis_size("example") // 2
    turns = owner.shape[0]
    rows, coords = train_grads.shape
    queries = query_cache.shape[1]
    lanes, delay = LANES, DELAY
    pieces = coords // lanes
    half = groups * pieces // 2
    steps = half + ring // 2 * delay
    sent = steps - delay
    cfg = (groups, ring, turns, rows, coords, steps, half, lanes, delay)
    bf16, f32 = jnp.bfloat16, jnp.float32
    dma = pltpu.SemaphoreType.DMA
    return pl.pallas_call(
        functools.partial(kernel, cfg),
        out_shape=jax.ShapeDtypeStruct((queries // groups, turns, rows), f32),
        in_specs=[
            pl.BlockSpec(memory_space=pl.ANY),
            pl.BlockSpec(memory_space=pl.ANY),
            pl.BlockSpec(memory_space=pltpu.VMEM),
            pl.BlockSpec(memory_space=pltpu.VMEM),
            pl.BlockSpec(memory_space=pltpu.SMEM),
            pl.BlockSpec(memory_space=pltpu.SMEM),
        ],
        out_specs=pl.BlockSpec(memory_space=pltpu.VMEM),
        scratch_shapes=[
            pltpu.VMEM((queries, coords), bf16),
            pltpu.VMEM((pieces, rows, lanes), bf16),
            pltpu.VMEM((32, 1024), f32),
            pltpu.VMEM((32, 1024), f32),
            pltpu.VMEM((1024, 1024), bf16),
            pltpu.VMEM((1024, 1024), bf16),
            pltpu.VMEM((groups, pieces, 16, lanes), bf16),
            pltpu.VMEM((groups, pieces, 16, lanes), bf16),
            pltpu.VMEM((2 * sent, turns, 16, lanes), bf16),
            pltpu.VMEM((2 * steps, turns, 16, lanes), bf16),
            pltpu.VMEM((2, 16 * turns, rows), f32),
            pltpu.VMEM((16 * turns, rows), f32),
            pltpu.VMEM((groups, 16 * turns, rows), bf16),
            pltpu.VMEM((groups, 16 * turns, rows), bf16),
            dma((1 + pieces,)),
            dma((groups,)),
            dma((groups,)),
            dma((2 * sent,)),
            dma((2 * sent,)),
            dma((groups,)),
            dma((groups,)),
        ],
        compiler_params=pltpu.CompilerParams(
            collective_id=0, has_side_effects=True, vmem_limit_bytes=56 * 1024 * 1024
        ),
    )(train_grads, query_cache, left_inverse, right_inverse, module_of, owner)


def solution(mesh):
    placed = (P("example", "param"), P("example", None, "param"), P(), P(), P(), P())
    return jax.shard_map(
        body, mesh=mesh, in_specs=placed, out_specs=P("param", None, "example"), check_vma=False
    )
```

```python
import functools
import math

import jax
import jax.numpy as jnp
from jax import lax
from jax.experimental import pallas as pl
from jax.experimental.pallas import tpu as pltpu
from jax.sharding import PartitionSpec as P

LANES = 256
PIECES = 4
BLOCK = LANES * PIECES
GROUPS = 16
BATCH = 4
TILE = 256
PARCEL = 128
MESH = pl.DeviceIdType.MESH
BF16, F32 = jnp.bfloat16, jnp.float32
ACROSS = (((1,), (1,)), ((), ()))


def kernel(
    ring,
    turns,
    train_hbm,
    query_hbm,
    left_ref,
    right_ref,
    module_ref,
    owner_ref,
    out_ref,
    query,
    train,
    spread_left,
    spread_right,
    kron_high,
    kron_low,
    swapper,
    mine,
    other,
    landed,
    passed,
    gathered,
    sorted_rows,
    product,
    summed,
    crossed,
    ordered,
    outgoing,
    incoming,
    load_sem,
    swap_send,
    swap_recv,
    train_send,
    train_recv,
    ring_send,
    ring_recv,
    sum_send,
    sum_recv,
    cross_send,
    cross_recv,
):
    owners = lax.axis_size("param")
    param = lax.axis_index("param")
    example = lax.axis_index("example")
    plane = lax.div(example, 2)
    side = lax.rem(example, 2)
    partner = plane * 2 + 1 - side
    following = lax.rem(plane + 1, ring) * 2 + side
    previous = lax.rem(plane + ring - 1, ring) * 2 + side
    reach = ring // 2
    laps = GROUPS // 2 + reach
    steps = laps * PIECES
    sent = steps - PIECES
    batches = GROUPS // BATCH
    own_tiles = train_hbm.shape[0] // TILE
    tiles = 2 * own_tiles

    barrier = pltpu.get_barrier_semaphore()
    for place in (partner, following, previous):
        pl.semaphore_signal(
            barrier, inc=1, device_id={"example": place}, device_id_type=MESH
        )

    @pl.loop(1, owners)
    def _(hop):
        pl.semaphore_signal(
            barrier,
            inc=1,
            device_id={"param": lax.rem(param + hop, owners)},
            device_id_type=MESH,
        )

    load_query = pltpu.make_async_copy(query_hbm.at[0], query, load_sem.at[0])
    load_query.start()
    here_lanes = pl.ds(pl.multiple_of(side * BLOCK, BLOCK), BLOCK)
    there_lanes = pl.ds(pl.multiple_of((1 - side) * BLOCK, BLOCK), BLOCK)
    load_train = [
        pltpu.make_async_copy(
            train_hbm.at[pl.ds(j * TILE, TILE), here_lanes], train.at[j], load_sem.at[1 + j]
        )
        for j in range(own_tiles)
    ]
    for copy in load_train:
        copy.start()
    parcels = own_tiles * (TILE // PARCEL)

    def give_train(i):
        return pltpu.make_async_remote_copy(
            src_ref=train_hbm.at[pl.ds(pl.multiple_of(i * PARCEL, PARCEL), PARCEL), there_lanes],
            dst_ref=train.at[
                own_tiles + lax.div(i, TILE // PARCEL),
                pl.ds(pl.multiple_of(lax.rem(i, TILE // PARCEL) * PARCEL, PARCEL), PARCEL),
            ],
            send_sem=train_send.at[i],
            recv_sem=train_recv.at[i],
            device_id={"example": partner},
            device_id_type=MESH,
        )

    row = lax.broadcasted_iota(jnp.int32, (256, 256), 0)
    col = lax.broadcasted_iota(jnp.int32, (256, 256), 1)
    swapper[...] = (lax.bitwise_and(col, 15) * 16 + lax.shift_right_logical(col, 4) == row).astype(
        F32
    ).astype(BF16)

    factor = 1.0 / math.sqrt(2 * BLOCK * owners)
    col = lax.broadcasted_iota(jnp.int32, (32, BLOCK), 1)
    row = lax.broadcasted_iota(jnp.int32, (32, BLOCK), 0)
    pick_outer = (lax.shift_right_logical(col, 5) == row).astype(F32)
    pick_inner = (lax.bitwise_and(col, 31) == row).astype(F32)
    for block in range(2):
        module = module_ref[param * 2 + block]
        spread_left[...] = lax.dot_general(
            left_ref[module] * factor,
            pick_outer,
            (((0,), (0,)), ((), ())),
            precision=lax.Precision.HIGHEST,
            preferred_element_type=F32,
        )
        spread_right[...] = lax.dot_general(
            right_ref[module],
            pick_inner,
            (((1,), (0,)), ((), ())),
            precision=lax.Precision.HIGHEST,
            preferred_element_type=F32,
        )

        @pl.loop(0, 32)
        def _(b):
            exact = spread_left[pl.ds(b, 1), :] * spread_right[...]
            high = exact.astype(BF16)
            low = (exact - high.astype(F32)).astype(BF16)
            at = pl.ds(pl.multiple_of(b * 32, 32), 32)
            kron_high[at, :] = high
            kron_low[at, :] = low

        if block == 0:
            pl.semaphore_wait(barrier, owners + 2)
            give_train(0).start()
            load_query.wait()
        source = jnp.dot(
            swapper[...], query[:, block * BLOCK : (block + 1) * BLOCK], preferred_element_type=F32
        ).astype(BF16)
        for k in range(BLOCK // TILE):
            cut = slice(k * TILE, (k + 1) * TILE)
            mixed = jnp.dot(source, kron_high[:, cut], preferred_element_type=F32) + jnp.dot(
                source, kron_low[:, cut], preferred_element_type=F32
            )
            mixed = mixed.astype(BF16)
            for part in range(TILE // LANES):
                mine[block, :, k * (TILE // LANES) + part] = mixed[
                    :, part * LANES : (part + 1) * LANES
                ].reshape(GROUPS, 16, LANES)

    def swap(order):
        return pltpu.make_async_remote_copy(
            src_ref=mine.at[1 - side, order],
            dst_ref=other.at[order],
            send_sem=swap_send.at[order],
            recv_sem=swap_recv.at[order],
            device_id={"example": partner},
            device_id_type=MESH,
        )

    @pl.loop(0, GROUPS // 2)
    def _(j):
        swap(j).start()
        swap(GROUPS - 1 - j).start()

    @pl.loop(1, parcels)
    def _(i):
        give_train(i).start()

    roots = [lax.div(owner_ref[t], 2) for t in range(turns)]
    sides = [lax.rem(owner_ref[t], 2) for t in range(turns)]
    ahead = [lax.rem(plane - r + ring, ring) for r in roots]
    near = [jnp.where(a <= reach, 0, 1) for a in ahead]
    far_off = [jnp.where(a <= reach, a, ring - a) for a in ahead]
    spare = [reach - f for f in far_off]

    def ring_copy(way, s):
        return pltpu.make_async_remote_copy(
            src_ref=passed.at[way * steps + s],
            dst_ref=landed.at[way * sent + s],
            send_sem=ring_send.at[way * sent + s],
            recv_sem=ring_recv.at[way * sent + s],
            device_id={"example": following if way == 0 else previous},
            device_id_type=MESH,
        )

    def advance(s, first, last):
        j = lax.div(s, PIECES)
        k = lax.rem(s, PIECES)

        @pl.when(jnp.logical_and(k == 0, j < GROUPS // 2))
        def _():
            swap(j).wait_recv()
            swap(GROUPS - 1 - j).wait_recv()

        for way in range(2):
            order = j if way == 0 else GROUPS - 1 - j
            here = mine[side, order, k]
            there = other[order, k]
            if not first:
                ring_copy(way, s - PIECES).wait_recv()
            for t in range(turns):
                value = jnp.where(sides[t] == side, here, there)
                if not first:
                    value = jnp.where(
                        ahead[t] == 0, value, landed[way * sent + s - PIECES, t]
                    )
                passed[way * steps + s, t] = value
            if not last:
                ring_copy(way, s).start()

    def gather(b):
        for u in range(BATCH):
            v = BATCH * b + u
            w = (BATCH // 2) * b + u // 2
            for t in range(turns):
                early = v < 2 * spare[t]
                if u % 2 == 0:
                    way = near[t]
                    lap = jnp.where(early, v, spare[t] + w) + far_off[t]
                else:
                    way = jnp.where(early, near[t], 1 - near[t])
                    lap = jnp.where(early, v + far_off[t], w - spare[t] + ring - far_off[t])
                base = way * steps + lap * PIECES
                for k in range(PIECES):
                    gathered[
                        (u * turns + t) * 16 : (u * turns + t + 1) * 16,
                        k * LANES : (k + 1) * LANES,
                    ] = passed[base + k, t]
        sorted_rows[...] = jnp.dot(
            swapper[...], gathered[...], preferred_element_type=F32
        ).astype(BF16)

    def multiply(b, j):
        product[...] = lax.dot_general(
            sorted_rows[...], train[j], ACROSS, preferred_element_type=F32
        )
        outgoing[b, :, j] = product[...].astype(BF16).reshape(owners, 16, TILE)
        summed[b, j] = product[pl.ds(pl.multiple_of(param * 16, 16), 16), :]

    def sum_copy(b, hop):
        return pltpu.make_async_remote_copy(
            src_ref=outgoing.at[b, lax.rem(param + hop, owners)],
            dst_ref=incoming.at[b, hop],
            send_sem=sum_send.at[b, hop],
            recv_sem=sum_recv.at[b, hop],
            device_id={"param": lax.rem(param + hop, owners)},
            device_id_type=MESH,
        )

    def give(b):
        @pl.loop(1, owners)
        def _(hop):
            sum_copy(b, hop).start()

    def cross(b):
        return pltpu.make_async_remote_copy(
            src_ref=summed.at[b, pl.ds(own_tiles, own_tiles)],
            dst_ref=crossed.at[b],
            send_sem=cross_send.at[b],
            recv_sem=cross_recv.at[b],
            device_id={"example": partner},
            device_id_type=MESH,
        )

    def finish(b):
        @pl.loop(1, owners)
        def _(hop):
            sum_copy(b, hop).wait_recv()
            summed[b] += incoming[b, hop].astype(F32)

        cross(b).start()

    start = (reach + 2) * PIECES

    @pl.loop(0, PIECES)
    def _(s):
        advance(s, True, False)

    @pl.loop(PIECES, start)
    def _(s):
        advance(s, False, False)

    for copy in load_train:
        copy.wait()

    @pl.loop(start, sent)
    def _(s):
        advance(s, False, False)
        lap = lax.div(s - start, PIECES)
        k = lax.rem(s, PIECES)
        b = lax.div(lap, 2)
        turn_of_batch = lax.rem(lap, 2) == 0

        @pl.when(jnp.logical_and(turn_of_batch, k == 0))
        def _():
            gather(b)

        @pl.when(jnp.logical_and(turn_of_batch, k == 1))
        def _():
            @pl.loop(0, own_tiles)
            def _(j):
                multiply(b, j)

        @pl.when(jnp.logical_and(turn_of_batch, k == 2))
        def _():
            @pl.when(b == 0)
            def _():
                @pl.loop(0, parcels)
                def _(i):
                    give_train(i).wait_recv()

            @pl.loop(own_tiles, tiles)
            def _(j):
                multiply(b, j)

        @pl.when(jnp.logical_and(turn_of_batch, k == PIECES - 1))
        def _():
            give(b)

    @pl.loop(sent, steps)
    def _(s):
        advance(s, False, True)

    gather(batches - 1)

    @pl.loop(0, tiles)
    def _(j):
        multiply(batches - 1, j)

    give(batches - 1)

    @pl.loop(0, batches)
    def _(b):
        finish(b)

    @pl.loop(0, sent)
    def _(s):
        ring_copy(0, s).wait_send()
        ring_copy(1, s).wait_send()

    @pl.loop(0, GROUPS)
    def _(order):
        swap(order).wait_send()

    @pl.loop(0, parcels)
    def _(i):
        give_train(i).wait_send()

    @pl.loop(0, batches)
    def _(b):
        @pl.loop(1, owners)
        def _(hop):
            sum_copy(b, hop).wait_send()

    for b in range(batches):
        cross(b).wait()
        for j in range(own_tiles):
            ordered[j, b * 16 : (b + 1) * 16, :] = summed[b, j] + crossed[b, j]

    for t in range(turns):

        @pl.loop(0, GROUPS)
        def _(i):
            a = jnp.where(near[t] == 0, i, GROUPS - 1 - i)
            v = jnp.where(
                a < 2 * spare[t],
                a,
                jnp.where(
                    a < GROUPS // 2 + spare[t],
                    2 * (a - spare[t]),
                    2 * (GROUPS - 1 - a + spare[t]) + 1,
                ),
            )
            for j in range(own_tiles):
                out_ref[i, t : t + 1, j * TILE : (j + 1) * TILE] = ordered[
                    j, pl.ds(v * turns + t, 1), :
                ]


def body(train_grads, query_cache, left_inverse, right_inverse, module_of, owner):
    owners = lax.axis_size("param")
    ring = lax.axis_size("example") // 2
    turns = owner.shape[0]
    rows, coords = train_grads.shape
    queries = query_cache.shape[1]
    own_tiles = rows // TILE
    batches = GROUPS // BATCH
    steps = (GROUPS // 2 + ring // 2) * PIECES
    sent = steps - PIECES
    dma = pltpu.SemaphoreType.DMA
    return pl.pallas_call(
        functools.partial(kernel, ring, turns),
        out_shape=jax.ShapeDtypeStruct((queries // owners, turns, rows), F32),
        in_specs=[
            pl.BlockSpec(memory_space=pl.ANY),
            pl.BlockSpec(memory_space=pl.ANY),
            pl.BlockSpec(memory_space=pltpu.VMEM),
            pl.BlockSpec(memory_space=pltpu.VMEM),
            pl.BlockSpec(memory_space=pltpu.SMEM),
            pl.BlockSpec(memory_space=pltpu.SMEM),
        ],
        out_specs=pl.BlockSpec(memory_space=pltpu.VMEM),
        scratch_shapes=[
            pltpu.VMEM((queries, coords), BF16),
            pltpu.VMEM((2 * own_tiles, TILE, BLOCK), BF16),
            pltpu.VMEM((32, BLOCK), F32),
            pltpu.VMEM((32, BLOCK), F32),
            pltpu.VMEM((BLOCK, BLOCK), BF16),
            pltpu.VMEM((BLOCK, BLOCK), BF16),
            pltpu.VMEM((256, 256), BF16),
            pltpu.VMEM((2, GROUPS, PIECES, 16, LANES), BF16),
            pltpu.VMEM((GROUPS, PIECES, 16, LANES), BF16),
            pltpu.VMEM((2 * sent, turns, 16, LANES), BF16),
            pltpu.VMEM((2 * steps, turns, 16, LANES), BF16),
            pltpu.VMEM((256, BLOCK), BF16),
            pltpu.VMEM((256, BLOCK), BF16),
            pltpu.VMEM((256, TILE), F32),
            pltpu.VMEM((batches, 2 * own_tiles, 16, TILE), F32),
            pltpu.VMEM((batches, own_tiles, 16, TILE), F32),
            pltpu.VMEM((own_tiles, 16 * batches, TILE), F32),
            pltpu.VMEM((batches, owners, 2 * own_tiles, 16, TILE), BF16),
            pltpu.VMEM((batches, owners, 2 * own_tiles, 16, TILE), BF16),
            dma((1 + own_tiles,)),
            dma((GROUPS,)),
            dma((GROUPS,)),
            dma((rows // PARCEL,)),
            dma((rows // PARCEL,)),
            dma((2 * sent,)),
            dma((2 * sent,)),
            dma((batches, owners)),
            dma((batches, owners)),
            dma((batches,)),
            dma((batches,)),
        ],
        compiler_params=pltpu.CompilerParams(
            collective_id=0, has_side_effects=True, vmem_limit_bytes=56 * 1024 * 1024
        ),
    )(train_grads, query_cache, left_inverse, right_inverse, module_of, owner)


def solution(mesh):
    placed = (P("example", "param"), P("example", None, "param"), P(), P(), P(), P())
    return jax.shard_map(
        body, mesh=mesh, in_specs=placed, out_specs=P("param", None, "example"), check_vma=False
    )
```

```python
import functools
import math

import jax
import jax.numpy as jnp
from jax import lax
from jax.experimental import pallas as pl
from jax.experimental.pallas import tpu as pltpu
from jax.sharding import PartitionSpec as P

LANES = 256
PIECES = 4
BLOCK = LANES * PIECES
GROUPS = 16
BATCH = 4
TILE = 256
PARCEL = 128
MESH = pl.DeviceIdType.MESH
BF16, F32 = jnp.bfloat16, jnp.float32
ACROSS = (((1,), (1,)), ((), ()))


def kernel(
    ring,
    turns,
    train_hbm,
    query_hbm,
    left_ref,
    right_ref,
    module_ref,
    owner_ref,
    out_ref,
    query,
    train,
    spread_left,
    spread_right,
    kron_high,
    kron_low,
    swapper,
    regroup,
    mine,
    other,
    landed,
    passed,
    gathered,
    sorted_rows,
    product,
    paired,
    summed,
    crossed,
    ordered,
    outgoing,
    incoming,
    load_sem,
    swap_send,
    swap_recv,
    train_send,
    train_recv,
    ring_send,
    ring_recv,
    pair_send,
    pair_recv,
    sum_send,
    sum_recv,
    cross_send,
    cross_recv,
):
    owners = lax.axis_size("param")
    param = lax.axis_index("param")
    example = lax.axis_index("example")
    chips = owners // 2
    chip = lax.div(param, 2)
    core = lax.rem(param, 2)
    sibling = chip * 2 + 1 - core
    plane = lax.div(example, 2)
    side = lax.rem(example, 2)
    partner = plane * 2 + 1 - side
    following = lax.rem(plane + 1, ring) * 2 + side
    previous = lax.rem(plane + ring - 1, ring) * 2 + side
    reach = ring // 2
    laps = GROUPS // 2 + reach
    steps = laps * PIECES
    sent = steps - PIECES
    batches = GROUPS // BATCH
    own_tiles = train_hbm.shape[0] // TILE

    barrier = pltpu.get_barrier_semaphore()
    for place in (partner, following, previous):
        pl.semaphore_signal(
            barrier, inc=1, device_id={"example": place}, device_id_type=MESH
        )

    pl.semaphore_signal(barrier, inc=1, device_id={"param": sibling}, device_id_type=MESH)

    @pl.loop(1, chips)
    def _(hop):
        pl.semaphore_signal(
            barrier,
            inc=1,
            device_id={"param": lax.rem(chip + hop, chips) * 2 + core},
            device_id_type=MESH,
        )

    load_query = pltpu.make_async_copy(query_hbm.at[0], query, load_sem.at[0])
    load_query.start()
    here_lanes = pl.ds(pl.multiple_of(side * BLOCK, BLOCK), BLOCK)
    there_lanes = pl.ds(pl.multiple_of((1 - side) * BLOCK, BLOCK), BLOCK)
    load_train = [
        pltpu.make_async_copy(
            train_hbm.at[pl.ds(j * TILE, TILE), here_lanes], train.at[j], load_sem.at[1 + j]
        )
        for j in range(own_tiles)
    ]
    for copy in load_train:
        copy.start()
    parcels = own_tiles * (TILE // PARCEL)

    def give_train(i):
        return pltpu.make_async_remote_copy(
            src_ref=train_hbm.at[pl.ds(pl.multiple_of(i * PARCEL, PARCEL), PARCEL), there_lanes],
            dst_ref=train.at[
                own_tiles + lax.div(i, TILE // PARCEL),
                pl.ds(pl.multiple_of(lax.rem(i, TILE // PARCEL) * PARCEL, PARCEL), PARCEL),
            ],
            send_sem=train_send.at[i],
            recv_sem=train_recv.at[i],
            device_id={"example": partner},
            device_id_type=MESH,
        )

    row = lax.broadcasted_iota(jnp.int32, (256, 256), 0)
    col = lax.broadcasted_iota(jnp.int32, (256, 256), 1)
    swapper[...] = (lax.bitwise_and(col, 15) * 16 + lax.shift_right_logical(col, 4) == row).astype(
        F32
    ).astype(BF16)
    group_row = lax.bitwise_and(col, 15)
    regroup[...] = (
        lax.bitwise_and(group_row, 1) * (chips * 16)
        + lax.shift_right_logical(group_row, 1) * 16
        + lax.shift_right_logical(col, 4)
        == row
    ).astype(F32).astype(BF16)

    def swap(order):
        return pltpu.make_async_remote_copy(
            src_ref=mine.at[1 - side, order],
            dst_ref=other.at[order],
            send_sem=swap_send.at[order],
            recv_sem=swap_recv.at[order],
            device_id={"example": partner},
            device_id_type=MESH,
        )

    factor = 1.0 / math.sqrt(2 * BLOCK * owners)
    col = lax.broadcasted_iota(jnp.int32, (32, BLOCK), 1)
    row = lax.broadcasted_iota(jnp.int32, (32, BLOCK), 0)
    pick_outer = (lax.shift_right_logical(col, 5) == row).astype(F32)
    pick_inner = (lax.bitwise_and(col, 31) == row).astype(F32)
    for block, first in ((1 - side, True), (side, False)):
        module = module_ref[param * 2 + block]
        spread_left[...] = lax.dot_general(
            left_ref[module] * factor,
            pick_outer,
            (((0,), (0,)), ((), ())),
            precision=lax.Precision.HIGHEST,
            preferred_element_type=F32,
        )
        spread_right[...] = lax.dot_general(
            right_ref[module],
            pick_inner,
            (((1,), (0,)), ((), ())),
            precision=lax.Precision.HIGHEST,
            preferred_element_type=F32,
        )

        @pl.loop(0, 32)
        def _(b):
            exact = spread_left[pl.ds(b, 1), :] * spread_right[...]
            high = exact.astype(BF16)
            low = (exact - high.astype(F32)).astype(BF16)
            at = pl.ds(pl.multiple_of(b * 32, 32), 32)
            kron_high[at, :] = high
            kron_low[at, :] = low

        if first:
            pl.semaphore_wait(barrier, chips + 3)
            give_train(0).start()
            load_query.wait()
        source = jnp.dot(
            swapper[...], query[:, pl.ds(pl.multiple_of(block * BLOCK, BLOCK), BLOCK)], preferred_element_type=F32
        ).astype(BF16)
        for k in range(BLOCK // TILE):
            cut = slice(k * TILE, (k + 1) * TILE)
            mixed = jnp.dot(source, kron_high[:, cut], preferred_element_type=F32) + jnp.dot(
                source, kron_low[:, cut], preferred_element_type=F32
            )
            mixed = mixed.astype(BF16)
            for part in range(TILE // LANES):
                mine[block, :, k * (TILE // LANES) + part] = mixed[
                    :, part * LANES : (part + 1) * LANES
                ].reshape(GROUPS, 16, LANES)
        if first:

            @pl.loop(0, GROUPS // 2)
            def _(j):
                swap(j).start()
                swap(GROUPS - 1 - j).start()

            @pl.loop(1, parcels)
            def _(i):
                give_train(i).start()

    roots = [lax.div(owner_ref[t], 2) for t in range(turns)]
    sides = [lax.rem(owner_ref[t], 2) for t in range(turns)]
    ahead = [lax.rem(plane - r + ring, ring) for r in roots]
    near = [jnp.where(a <= reach, 0, 1) for a in ahead]
    far_off = [jnp.where(a <= reach, a, ring - a) for a in ahead]
    spare = [reach - f for f in far_off]

    def ring_copy(way, s):
        return pltpu.make_async_remote_copy(
            src_ref=passed.at[way * steps + s],
            dst_ref=landed.at[way * sent + s],
            send_sem=ring_send.at[way * sent + s],
            recv_sem=ring_recv.at[way * sent + s],
            device_id={"example": following if way == 0 else previous},
            device_id_type=MESH,
        )

    def advance(s, first, last):
        j = lax.div(s, PIECES)
        k = lax.rem(s, PIECES)

        @pl.when(jnp.logical_and(k == 0, j < GROUPS // 2))
        def _():
            swap(j).wait_recv()
            swap(GROUPS - 1 - j).wait_recv()

        for way in range(2):
            order = j if way == 0 else GROUPS - 1 - j
            here = mine[side, order, k]
            there = other[order, k]
            if not first:
                ring_copy(way, s - PIECES).wait()
            for t in range(turns):
                value = jnp.where(sides[t] == side, here, there)
                if not first:
                    value = jnp.where(
                        ahead[t] == 0, value, landed[way * sent + s - PIECES, t]
                    )
                passed[way * steps + s, t] = value
            if not last:
                ring_copy(way, s).start()

    def gather(b):
        for u in range(BATCH):
            v = BATCH * b + u
            w = (BATCH // 2) * b + u // 2
            for t in range(turns):
                early = v < 2 * spare[t]
                if u % 2 == 0:
                    way = near[t]
                    lap = jnp.where(early, v, spare[t] + w) + far_off[t]
                else:
                    way = jnp.where(early, near[t], 1 - near[t])
                    lap = jnp.where(early, v + far_off[t], w - spare[t] + ring - far_off[t])
                base = way * steps + lap * PIECES
                for k in range(PIECES):
                    gathered[
                        (u * turns + t) * 16 : (u * turns + t + 1) * 16,
                        k * LANES : (k + 1) * LANES,
                    ] = passed[base + k, t]
        sorted_rows[...] = jnp.dot(
            regroup[...], gathered[...], preferred_element_type=F32
        ).astype(BF16)

    def pair_copy(b, part):
        tiles_of = pl.ds(part * own_tiles, own_tiles)
        return pltpu.make_async_remote_copy(
            src_ref=product.at[b, 1 - core, tiles_of],
            dst_ref=paired.at[b, tiles_of],
            send_sem=pair_send.at[b, part],
            recv_sem=pair_recv.at[b, part],
            device_id={"param": sibling},
            device_id_type=MESH,
        )

    def multiply(b, part):
        @pl.loop(part * own_tiles, (part + 1) * own_tiles)
        def _(j):
            product[b, :, j] = lax.dot_general(
                sorted_rows[...], train[j], ACROSS, preferred_element_type=F32
            ).reshape(2, chips * 16, TILE)

        pair_copy(b, part).start()

    def sum_copy(b, part, hop):
        tiles_of = pl.ds(part * own_tiles, own_tiles)
        place = lax.rem(chip + hop, chips)
        return pltpu.make_async_remote_copy(
            src_ref=outgoing.at[b, place, tiles_of],
            dst_ref=incoming.at[b, hop, tiles_of],
            send_sem=sum_send.at[b, part, hop],
            recv_sem=sum_recv.at[b, part, hop],
            device_id={"param": place * 2 + core},
            device_id_type=MESH,
        )

    def give(b, part):
        pair_copy(b, part).wait_recv()

        @pl.loop(part * own_tiles, (part + 1) * own_tiles)
        def _(j):
            both = product[b, core, j] + paired[b, j]
            paired[b, j] = both
            outgoing[b, :, j] = both.astype(BF16).reshape(chips, 16, TILE)
            summed[b, j] = paired[b, j, pl.ds(pl.multiple_of(chip * 16, 16), 16), :]

        @pl.loop(1, chips)
        def _(hop):
            sum_copy(b, part, hop).start()

    def cross(b):
        return pltpu.make_async_remote_copy(
            src_ref=summed.at[b, pl.ds(own_tiles, own_tiles)],
            dst_ref=crossed.at[b],
            send_sem=cross_send.at[b],
            recv_sem=cross_recv.at[b],
            device_id={"example": partner},
            device_id_type=MESH,
        )

    def finish(b, part):
        tiles_of = pl.ds(part * own_tiles, own_tiles)

        @pl.loop(1, chips)
        def _(hop):
            sum_copy(b, part, hop).wait_recv()
            summed[b, tiles_of] += incoming[b, hop, tiles_of].astype(F32)

        if part == 1:
            cross(b).start()

    def settle(b):
        cross(b).wait_recv()
        for j in range(own_tiles):
            ordered[j, b * 16 : (b + 1) * 16, :] = summed[b, j] + crossed[b, j]

    start = (reach + 2) * PIECES

    @pl.loop(0, PIECES)
    def _(s):
        advance(s, True, False)

    @pl.loop(PIECES, start)
    def _(s):
        advance(s, False, False)

    for copy in load_train:
        copy.wait()

    @pl.loop(start, sent)
    def _(s):
        advance(s, False, False)
        lap = lax.div(s - start, PIECES)
        k = lax.rem(s, PIECES)
        b = lax.div(lap, 2)
        turn_of_batch = lax.rem(lap, 2) == 0

        @pl.when(jnp.logical_and(turn_of_batch, k == 0))
        def _():
            gather(b)

        @pl.when(jnp.logical_and(turn_of_batch, k == 1))
        def _():
            multiply(b, 0)

        @pl.when(jnp.logical_and(turn_of_batch, k == 2))
        def _():
            @pl.when(b == 0)
            def _():
                @pl.loop(0, parcels)
                def _(i):
                    give_train(i).wait_recv()

            multiply(b, 1)

        @pl.when(jnp.logical_and(turn_of_batch, k == 3))
        def _():
            give(b, 0)

        @pl.when(jnp.logical_and(jnp.logical_not(turn_of_batch), k == 0))
        def _():
            give(b, 1)

        @pl.when(jnp.logical_and(lap == 3, k == 2))
        def _():
            finish(0, 0)

        @pl.when(jnp.logical_and(lap == 3, k == 3))
        def _():
            finish(0, 1)

    @pl.loop(sent, steps)
    def _(s):
        advance(s, False, True)

        @pl.when(s == sent)
        def _():
            give(batches - 2, 1)

        @pl.when(s == steps - 2)
        def _():
            finish(1, 0)

        @pl.when(s == steps - 1)
        def _():
            finish(1, 1)

    gather(batches - 1)
    multiply(batches - 1, 1)
    multiply(batches - 1, 0)
    give(batches - 1, 1)
    give(batches - 1, 0)
    for b in range(2, batches - 1):
        finish(b, 1)
        finish(b, 0)
    for b in range(batches - 2):
        settle(b)
    finish(batches - 1, 1)
    settle(batches - 2)
    finish(batches - 1, 0)

    @pl.loop(0, GROUPS)
    def _(order):
        swap(order).wait_send()

    @pl.loop(0, parcels)
    def _(i):
        give_train(i).wait_send()

    for part in range(2):

        @pl.loop(0, batches)
        def _(b):
            pair_copy(b, part).wait_send()

            @pl.loop(1, chips)
            def _(hop):
                sum_copy(b, part, hop).wait_send()

    settle(batches - 1)

    @pl.loop(0, batches)
    def _(b):
        cross(b).wait_send()

    for t in range(turns):

        @pl.loop(0, GROUPS)
        def _(i):
            a = jnp.where(near[t] == 0, i, GROUPS - 1 - i)
            v = jnp.where(
                a < 2 * spare[t],
                a,
                jnp.where(
                    a < GROUPS // 2 + spare[t],
                    2 * (a - spare[t]),
                    2 * (GROUPS - 1 - a + spare[t]) + 1,
                ),
            )
            for j in range(own_tiles):
                out_ref[i, t : t + 1, j * TILE : (j + 1) * TILE] = ordered[
                    j, pl.ds(v * turns + t, 1), :
                ]


def body(train_grads, query_cache, left_inverse, right_inverse, module_of, owner):
    owners = lax.axis_size("param")
    ring = lax.axis_size("example") // 2
    turns = owner.shape[0]
    rows, coords = train_grads.shape
    queries = query_cache.shape[1]
    own_tiles = rows // TILE
    batches = GROUPS // BATCH
    steps = (GROUPS // 2 + ring // 2) * PIECES
    sent = steps - PIECES
    dma = pltpu.SemaphoreType.DMA
    return pl.pallas_call(
        functools.partial(kernel, ring, turns),
        out_shape=jax.ShapeDtypeStruct((queries // owners, turns, rows), F32),
        in_specs=[
            pl.BlockSpec(memory_space=pl.ANY),
            pl.BlockSpec(memory_space=pl.ANY),
            pl.BlockSpec(memory_space=pltpu.VMEM),
            pl.BlockSpec(memory_space=pltpu.VMEM),
            pl.BlockSpec(memory_space=pltpu.SMEM),
            pl.BlockSpec(memory_space=pltpu.SMEM),
        ],
        out_specs=pl.BlockSpec(memory_space=pltpu.VMEM),
        scratch_shapes=[
            pltpu.VMEM((queries, coords), BF16),
            pltpu.VMEM((2 * own_tiles, TILE, BLOCK), BF16),
            pltpu.VMEM((32, BLOCK), F32),
            pltpu.VMEM((32, BLOCK), F32),
            pltpu.VMEM((BLOCK, BLOCK), BF16),
            pltpu.VMEM((BLOCK, BLOCK), BF16),
            pltpu.VMEM((256, 256), BF16),
            pltpu.VMEM((256, 256), BF16),
            pltpu.VMEM((2, GROUPS, PIECES, 16, LANES), BF16),
            pltpu.VMEM((GROUPS, PIECES, 16, LANES), BF16),
            pltpu.VMEM((2 * sent, turns, 16, LANES), BF16),
            pltpu.VMEM((2 * steps, turns, 16, LANES), BF16),
            pltpu.VMEM((256, BLOCK), BF16),
            pltpu.VMEM((256, BLOCK), BF16),
            pltpu.VMEM((batches, 2, 2 * own_tiles, 8 * owners, TILE), F32),
            pltpu.VMEM((batches, 2 * own_tiles, 8 * owners, TILE), F32),
            pltpu.VMEM((batches, 2 * own_tiles, 16, TILE), F32),
            pltpu.VMEM((batches, own_tiles, 16, TILE), F32),
            pltpu.VMEM((own_tiles, 16 * batches, TILE), F32),
            pltpu.VMEM((batches, owners // 2, 2 * own_tiles, 16, TILE), BF16),
            pltpu.VMEM((batches, owners // 2, 2 * own_tiles, 16, TILE), BF16),
            dma((1 + own_tiles,)),
            dma((GROUPS,)),
            dma((GROUPS,)),
            dma((rows // PARCEL,)),
            dma((rows // PARCEL,)),
            dma((2 * sent,)),
            dma((2 * sent,)),
            dma((batches, 2)),
            dma((batches, 2)),
            dma((batches, 2, owners // 2)),
            dma((batches, 2, owners // 2)),
            dma((batches,)),
            dma((batches,)),
        ],
        compiler_params=pltpu.CompilerParams(
            collective_id=0, has_side_effects=True, vmem_limit_bytes=56 * 1024 * 1024
        ),
    )(train_grads, query_cache, left_inverse, right_inverse, module_of, owner)


def solution(mesh):
    placed = (P("example", "param"), P("example", None, "param"), P(), P(), P(), P())
    return jax.shard_map(
        body, mesh=mesh, in_specs=placed, out_specs=P("param", None, "example"), check_vma=False
    )
```

```python
import functools
import math

import jax
import jax.numpy as jnp
from jax import lax
from jax.experimental import pallas as pl
from jax.experimental.pallas import tpu as pltpu
from jax.sharding import PartitionSpec as P

LANES = 256
PIECES = 4
BLOCK = LANES * PIECES
GROUPS = 16
BATCH = 4
TILE = 256
PARCEL = 64
MESH = pl.DeviceIdType.MESH
BF16, F32 = jnp.bfloat16, jnp.float32
ACROSS = (((1,), (1,)), ((), ()))


def kernel(
    ring,
    turns,
    train_hbm,
    query_hbm,
    left_ref,
    right_ref,
    module_ref,
    owner_ref,
    out_ref,
    query,
    train,
    spread_left,
    spread_right,
    kron_high,
    kron_low,
    swapper,
    regroup,
    mine,
    other,
    landed,
    passed,
    gathered,
    sorted_rows,
    product,
    paired,
    summed,
    crossed,
    ordered,
    outgoing,
    incoming,
    load_sem,
    swap_send,
    swap_recv,
    train_send,
    train_recv,
    ring_send,
    ring_recv,
    pair_send,
    pair_recv,
    sum_send,
    sum_recv,
    cross_send,
    cross_recv,
):
    owners = lax.axis_size("param")
    param = lax.axis_index("param")
    example = lax.axis_index("example")
    chips = owners // 2
    chip = lax.div(param, 2)
    core = lax.rem(param, 2)
    sibling = chip * 2 + 1 - core
    plane = lax.div(example, 2)
    side = lax.rem(example, 2)
    partner = plane * 2 + 1 - side
    following = lax.rem(plane + 1, ring) * 2 + side
    previous = lax.rem(plane + ring - 1, ring) * 2 + side
    reach = ring // 2
    laps = GROUPS // 2 + reach
    steps = laps * PIECES
    sent = steps - PIECES
    batches = GROUPS // BATCH
    own_tiles = train_hbm.shape[0] // TILE

    barrier = pltpu.get_barrier_semaphore()
    for place in (partner, following, previous):
        pl.semaphore_signal(
            barrier, inc=1, device_id={"example": place}, device_id_type=MESH
        )

    pl.semaphore_signal(barrier, inc=1, device_id={"param": sibling}, device_id_type=MESH)

    @pl.loop(1, chips)
    def _(hop):
        pl.semaphore_signal(
            barrier,
            inc=1,
            device_id={"param": lax.rem(chip + hop, chips) * 2 + core},
            device_id_type=MESH,
        )

    load_query = pltpu.make_async_copy(query_hbm.at[0], query, load_sem.at[0])
    load_query.start()
    here_lanes = pl.ds(pl.multiple_of(side * BLOCK, BLOCK), BLOCK)
    there_lanes = pl.ds(pl.multiple_of((1 - side) * BLOCK, BLOCK), BLOCK)
    load_train = [
        pltpu.make_async_copy(
            train_hbm.at[pl.ds(j * TILE, TILE), here_lanes], train.at[j], load_sem.at[1 + j]
        )
        for j in range(own_tiles)
    ]
    for copy in load_train:
        copy.start()
    parcels = own_tiles * (TILE // PARCEL)

    def give_train(i):
        return pltpu.make_async_remote_copy(
            src_ref=train_hbm.at[pl.ds(pl.multiple_of(i * PARCEL, PARCEL), PARCEL), there_lanes],
            dst_ref=train.at[
                own_tiles + lax.div(i, TILE // PARCEL),
                pl.ds(pl.multiple_of(lax.rem(i, TILE // PARCEL) * PARCEL, PARCEL), PARCEL),
            ],
            send_sem=train_send.at[i],
            recv_sem=train_recv.at[i],
            device_id={"example": partner},
            device_id_type=MESH,
        )

    row = lax.broadcasted_iota(jnp.int32, (256, 256), 0)
    col = lax.broadcasted_iota(jnp.int32, (256, 256), 1)
    swapper[...] = (lax.bitwise_and(col, 15) * 16 + lax.shift_right_logical(col, 4) == row).astype(
        F32
    ).astype(BF16)
    group_row = lax.bitwise_and(col, 15)
    regroup[...] = (
        lax.bitwise_and(group_row, 1) * (chips * 16)
        + lax.shift_right_logical(group_row, 1) * 16
        + lax.shift_right_logical(col, 4)
        == row
    ).astype(F32).astype(BF16)

    def swap(order):
        return pltpu.make_async_remote_copy(
            src_ref=mine.at[1 - side, order],
            dst_ref=other.at[order],
            send_sem=swap_send.at[order],
            recv_sem=swap_recv.at[order],
            device_id={"example": partner},
            device_id_type=MESH,
        )

    factor = 1.0 / math.sqrt(2 * BLOCK * owners)
    col = lax.broadcasted_iota(jnp.int32, (32, BLOCK), 1)
    row = lax.broadcasted_iota(jnp.int32, (32, BLOCK), 0)
    pick_outer = (lax.shift_right_logical(col, 5) == row).astype(F32)
    pick_inner = (lax.bitwise_and(col, 31) == row).astype(F32)
    for block, first in ((1 - side, True), (side, False)):
        module = module_ref[param * 2 + block]
        spread_left[...] = lax.dot_general(
            left_ref[module] * factor,
            pick_outer,
            (((0,), (0,)), ((), ())),
            precision=lax.Precision.HIGHEST,
            preferred_element_type=F32,
        )
        spread_right[...] = lax.dot_general(
            right_ref[module],
            pick_inner,
            (((1,), (0,)), ((), ())),
            precision=lax.Precision.HIGHEST,
            preferred_element_type=F32,
        )

        @pl.loop(0, 32)
        def _(b):
            exact = spread_left[pl.ds(b, 1), :] * spread_right[...]
            high = exact.astype(BF16)
            low = (exact - high.astype(F32)).astype(BF16)
            at = pl.ds(pl.multiple_of(b * 32, 32), 32)
            kron_high[at, :] = high
            kron_low[at, :] = low

        if first:
            pl.semaphore_wait(barrier, chips + 3)
            give_train(0).start()
            load_query.wait()
        source = jnp.dot(
            swapper[...], query[:, pl.ds(pl.multiple_of(block * BLOCK, BLOCK), BLOCK)], preferred_element_type=F32
        ).astype(BF16)
        for k in range(BLOCK // TILE):
            cut = slice(k * TILE, (k + 1) * TILE)
            mixed = jnp.dot(source, kron_high[:, cut], preferred_element_type=F32) + jnp.dot(
                source, kron_low[:, cut], preferred_element_type=F32
            )
            mixed = mixed.astype(BF16)
            for part in range(TILE // LANES):
                mine[block, :, k * (TILE // LANES) + part] = mixed[
                    :, part * LANES : (part + 1) * LANES
                ].reshape(GROUPS, 16, LANES)
        if first:

            @pl.loop(0, GROUPS // 2)
            def _(j):
                swap(j).start()
                swap(GROUPS - 1 - j).start()

            @pl.loop(1, parcels)
            def _(i):
                give_train(i).start()

    roots = [lax.div(owner_ref[t], 2) for t in range(turns)]
    sides = [lax.rem(owner_ref[t], 2) for t in range(turns)]
    ahead = [lax.rem(plane - r + ring, ring) for r in roots]
    near = [jnp.where(a <= reach, 0, 1) for a in ahead]
    far_off = [jnp.where(a <= reach, a, ring - a) for a in ahead]
    spare = [reach - f for f in far_off]

    def ring_copy(way, s):
        return pltpu.make_async_remote_copy(
            src_ref=passed.at[way * steps + s],
            dst_ref=landed.at[way * sent + s],
            send_sem=ring_send.at[way * sent + s],
            recv_sem=ring_recv.at[way * sent + s],
            device_id={"example": following if way == 0 else previous},
            device_id_type=MESH,
        )

    def advance(s, first, last):
        j = lax.div(s, PIECES)
        k = lax.rem(s, PIECES)

        @pl.when(jnp.logical_and(k == 0, j < GROUPS // 2))
        def _():
            swap(j).wait_recv()
            swap(GROUPS - 1 - j).wait_recv()

        for way in range(2):
            order = j if way == 0 else GROUPS - 1 - j
            here = mine[side, order, k]
            there = other[order, k]
            if not first:
                ring_copy(way, s - PIECES).wait()
            for t in range(turns):
                value = jnp.where(sides[t] == side, here, there)
                if not first:
                    value = jnp.where(
                        ahead[t] == 0, value, landed[way * sent + s - PIECES, t]
                    )
                passed[way * steps + s, t] = value
            if not last:
                ring_copy(way, s).start()

    def gather(b):
        for u in range(BATCH):
            v = BATCH * b + u
            w = (BATCH // 2) * b + u // 2
            for t in range(turns):
                early = v < 2 * spare[t]
                if u % 2 == 0:
                    way = near[t]
                    lap = jnp.where(early, v, spare[t] + w) + far_off[t]
                else:
                    way = jnp.where(early, near[t], 1 - near[t])
                    lap = jnp.where(early, v + far_off[t], w - spare[t] + ring - far_off[t])
                base = way * steps + lap * PIECES
                for k in range(PIECES):
                    gathered[
                        (u * turns + t) * 16 : (u * turns + t + 1) * 16,
                        k * LANES : (k + 1) * LANES,
                    ] = passed[base + k, t]

    def sort_rows():
        sorted_rows[...] = jnp.dot(
            regroup[...], gathered[...], preferred_element_type=F32
        ).astype(BF16)

    def pair_copy(b, part):
        tiles_of = pl.ds(part * own_tiles, own_tiles)
        return pltpu.make_async_remote_copy(
            src_ref=product.at[b, 1 - core, tiles_of],
            dst_ref=paired.at[b, tiles_of],
            send_sem=pair_send.at[b, part],
            recv_sem=pair_recv.at[b, part],
            device_id={"param": sibling},
            device_id_type=MESH,
        )

    def multiply(b, j):
        product[b, :, j] = lax.dot_general(
            sorted_rows[...], train[j], ACROSS, preferred_element_type=F32
        ).reshape(2, chips * 16, TILE)
        if j % own_tiles == own_tiles - 1:
            pair_copy(b, j // own_tiles).start()

    def sum_copy(b, part, hop):
        tiles_of = pl.ds(part * own_tiles, own_tiles)
        place = lax.rem(chip + hop, chips)
        return pltpu.make_async_remote_copy(
            src_ref=outgoing.at[b, place, tiles_of],
            dst_ref=incoming.at[b, hop, tiles_of],
            send_sem=sum_send.at[b, part, hop],
            recv_sem=sum_recv.at[b, part, hop],
            device_id={"param": place * 2 + core},
            device_id_type=MESH,
        )

    def give(b, part):
        pair_copy(b, part).wait_recv()

        @pl.loop(part * own_tiles, (part + 1) * own_tiles)
        def _(j):
            both = product[b, core, j] + paired[b, j]
            paired[b, j] = both
            outgoing[b, :, j] = both.astype(BF16).reshape(chips, 16, TILE)
            summed[b, j] = paired[b, j, pl.ds(pl.multiple_of(chip * 16, 16), 16), :]

        @pl.loop(1, chips)
        def _(hop):
            sum_copy(b, part, hop).start()

    def cross(b):
        return pltpu.make_async_remote_copy(
            src_ref=summed.at[b, pl.ds(own_tiles, own_tiles)],
            dst_ref=crossed.at[b],
            send_sem=cross_send.at[b],
            recv_sem=cross_recv.at[b],
            device_id={"example": partner},
            device_id_type=MESH,
        )

    def finish(b, part):
        tiles_of = pl.ds(part * own_tiles, own_tiles)

        @pl.loop(1, chips)
        def _(hop):
            sum_copy(b, part, hop).wait_recv()
            summed[b, tiles_of] += incoming[b, hop, tiles_of].astype(F32)

        if part == 1:
            cross(b).start()

    def settle(b):
        cross(b).wait_recv()
        for j in range(own_tiles):
            ordered[j, b * 16 : (b + 1) * 16, :] = summed[b, j] + crossed[b, j]

    start = (reach + 2) * PIECES

    @pl.loop(0, PIECES)
    def _(s):
        advance(s, True, False)

    @pl.loop(PIECES, start)
    def _(s):
        advance(s, False, False)

    for copy in load_train:
        copy.wait()

    def arrived(b, j):
        @pl.when(b == 0)
        def _():
            @pl.loop((j - own_tiles) * (TILE // PARCEL), (j - own_tiles + 1) * (TILE // PARCEL))
            def _(i):
                give_train(i).wait_recv()

    def work(s):
        b = lax.div(s - start, 2 * PIECES)
        k = lax.rem(s - start, 2 * PIECES)

        @pl.when(k == 0)
        def _():
            gather(b)

        @pl.when(k == 1)
        def _():
            sort_rows()
            multiply(b, 0)

        @pl.when(k == 2)
        def _():
            multiply(b, 1)
            multiply(b, 2)

        late = jnp.where(b == 0, 2, 0)

        @pl.when(k == 3 + late)
        def _():
            arrived(b, 3)
            multiply(b, 3)

        @pl.when(k == 4 + late)
        def _():
            arrived(b, 4)
            multiply(b, 4)
            arrived(b, 5)
            multiply(b, 5)

        @pl.when(k == 5 - late)
        def _():
            give(b, 0)

        @pl.when(k == jnp.where(b == 0, 7, 6))
        def _():
            give(b, 1)

        @pl.when(jnp.logical_and(k == 7, b > 0))
        def _():
            finish(b - 1, 1)
            finish(b - 1, 0)

    @pl.loop(start, sent)
    def _(s):
        advance(s, False, False)
        work(s)

    @pl.loop(sent, steps)
    def _(s):
        advance(s, False, True)
        work(s)

    gather(batches - 1)
    sort_rows()
    for j in range(own_tiles, 2 * own_tiles):
        multiply(batches - 1, j)
    multiply(batches - 1, 0)
    give(batches - 1, 1)
    for j in range(1, own_tiles):
        multiply(batches - 1, j)
    give(batches - 1, 0)
    for b in range(2, batches - 1):
        finish(b, 1)
        finish(b, 0)
    for b in range(batches - 2):
        settle(b)
    finish(batches - 1, 1)
    settle(batches - 2)
    finish(batches - 1, 0)

    @pl.loop(0, GROUPS)
    def _(order):
        swap(order).wait_send()

    @pl.loop(0, parcels)
    def _(i):
        give_train(i).wait_send()

    for part in range(2):

        @pl.loop(0, batches)
        def _(b):
            pair_copy(b, part).wait_send()

            @pl.loop(1, chips)
            def _(hop):
                sum_copy(b, part, hop).wait_send()

    settle(batches - 1)

    @pl.loop(0, batches)
    def _(b):
        cross(b).wait_send()

    for t in range(turns):

        @pl.loop(0, GROUPS)
        def _(i):
            a = jnp.where(near[t] == 0, i, GROUPS - 1 - i)
            v = jnp.where(
                a < 2 * spare[t],
                a,
                jnp.where(
                    a < GROUPS // 2 + spare[t],
                    2 * (a - spare[t]),
                    2 * (GROUPS - 1 - a + spare[t]) + 1,
                ),
            )
            for j in range(own_tiles):
                out_ref[i, t : t + 1, j * TILE : (j + 1) * TILE] = ordered[
                    j, pl.ds(v * turns + t, 1), :
                ]


def body(train_grads, query_cache, left_inverse, right_inverse, module_of, owner):
    owners = lax.axis_size("param")
    ring = lax.axis_size("example") // 2
    turns = owner.shape[0]
    rows, coords = train_grads.shape
    queries = query_cache.shape[1]
    own_tiles = rows // TILE
    batches = GROUPS // BATCH
    steps = (GROUPS // 2 + ring // 2) * PIECES
    sent = steps - PIECES
    dma = pltpu.SemaphoreType.DMA
    return pl.pallas_call(
        functools.partial(kernel, ring, turns),
        out_shape=jax.ShapeDtypeStruct((queries // owners, turns, rows), F32),
        in_specs=[
            pl.BlockSpec(memory_space=pl.ANY),
            pl.BlockSpec(memory_space=pl.ANY),
            pl.BlockSpec(memory_space=pltpu.VMEM),
            pl.BlockSpec(memory_space=pltpu.VMEM),
            pl.BlockSpec(memory_space=pltpu.SMEM),
            pl.BlockSpec(memory_space=pltpu.SMEM),
        ],
        out_specs=pl.BlockSpec(memory_space=pltpu.VMEM),
        scratch_shapes=[
            pltpu.VMEM((queries, coords), BF16),
            pltpu.VMEM((2 * own_tiles, TILE, BLOCK), BF16),
            pltpu.VMEM((32, BLOCK), F32),
            pltpu.VMEM((32, BLOCK), F32),
            pltpu.VMEM((BLOCK, BLOCK), BF16),
            pltpu.VMEM((BLOCK, BLOCK), BF16),
            pltpu.VMEM((256, 256), BF16),
            pltpu.VMEM((256, 256), BF16),
            pltpu.VMEM((2, GROUPS, PIECES, 16, LANES), BF16),
            pltpu.VMEM((GROUPS, PIECES, 16, LANES), BF16),
            pltpu.VMEM((2 * sent, turns, 16, LANES), BF16),
            pltpu.VMEM((2 * steps, turns, 16, LANES), BF16),
            pltpu.VMEM((256, BLOCK), BF16),
            pltpu.VMEM((256, BLOCK), BF16),
            pltpu.VMEM((batches, 2, 2 * own_tiles, 8 * owners, TILE), F32),
            pltpu.VMEM((batches, 2 * own_tiles, 8 * owners, TILE), F32),
            pltpu.VMEM((batches, 2 * own_tiles, 16, TILE), F32),
            pltpu.VMEM((batches, own_tiles, 16, TILE), F32),
            pltpu.VMEM((own_tiles, 16 * batches, TILE), F32),
            pltpu.VMEM((batches, owners // 2, 2 * own_tiles, 16, TILE), BF16),
            pltpu.VMEM((batches, owners // 2, 2 * own_tiles, 16, TILE), BF16),
            dma((1 + own_tiles,)),
            dma((GROUPS,)),
            dma((GROUPS,)),
            dma((rows // PARCEL,)),
            dma((rows // PARCEL,)),
            dma((2 * sent,)),
            dma((2 * sent,)),
            dma((batches, 2)),
            dma((batches, 2)),
            dma((batches, 2, owners // 2)),
            dma((batches, 2, owners // 2)),
            dma((batches,)),
            dma((batches,)),
        ],
        compiler_params=pltpu.CompilerParams(
            collective_id=0, has_side_effects=True, vmem_limit_bytes=56 * 1024 * 1024
        ),
    )(train_grads, query_cache, left_inverse, right_inverse, module_of, owner)


def solution(mesh):
    placed = (P("example", "param"), P("example", None, "param"), P(), P(), P(), P())
    return jax.shard_map(
        body, mesh=mesh, in_specs=placed, out_specs=P("param", None, "example"), check_vma=False
    )
```

```python
import functools
import math

import jax
import jax.numpy as jnp
from jax import lax
from jax.experimental import pallas as pl
from jax.experimental.pallas import tpu as pltpu
from jax.sharding import PartitionSpec as P

LANES = 256
PIECES = 4
BLOCK = LANES * PIECES
GROUPS = 16
BATCH = 4
TILE = 256
PARCEL = 64
MESH = pl.DeviceIdType.MESH
BF16, F32 = jnp.bfloat16, jnp.float32
ACROSS = (((1,), (1,)), ((), ()))


def kernel(
    ring,
    turns,
    train_hbm,
    query_hbm,
    left_hbm,
    right_hbm,
    module_ref,
    owner_ref,
    out_ref,
    left_ref,
    right_ref,
    query,
    train,
    spread_left,
    spread_right,
    kron_high,
    kron_low,
    swapper,
    regroup,
    mine,
    other,
    landed,
    passed,
    gathered,
    sorted_rows,
    product,
    paired,
    summed,
    crossed,
    ordered,
    outgoing,
    incoming,
    load_sem,
    swap_send,
    swap_recv,
    train_send,
    train_recv,
    ring_send,
    ring_recv,
    pair_send,
    pair_recv,
    sum_send,
    sum_recv,
    cross_send,
    cross_recv,
):
    owners = lax.axis_size("param")
    param = lax.axis_index("param")
    example = lax.axis_index("example")
    chips = owners // 2
    chip = lax.div(param, 2)
    core = lax.rem(param, 2)
    sibling = chip * 2 + 1 - core
    plane = lax.div(example, 2)
    side = lax.rem(example, 2)
    partner = plane * 2 + 1 - side
    following = lax.rem(plane + 1, ring) * 2 + side
    previous = lax.rem(plane + ring - 1, ring) * 2 + side
    reach = ring // 2
    laps = GROUPS // 2 + reach
    steps = laps * PIECES
    sent = steps - PIECES
    batches = GROUPS // BATCH
    own_tiles = train_hbm.shape[0] // TILE

    barrier = pltpu.get_barrier_semaphore()
    for place in (partner, following, previous):
        pl.semaphore_signal(
            barrier, inc=1, device_id={"example": place}, device_id_type=MESH
        )

    pl.semaphore_signal(barrier, inc=1, device_id={"param": sibling}, device_id_type=MESH)

    @pl.loop(1, chips)
    def _(hop):
        pl.semaphore_signal(
            barrier,
            inc=1,
            device_id={"param": lax.rem(chip + hop, chips) * 2 + core},
            device_id_type=MESH,
        )

    load_query = pltpu.make_async_copy(query_hbm.at[0], query, load_sem.at[0])
    load_query.start()
    load_sides = [
        pltpu.make_async_copy(left_hbm, left_ref, load_sem.at[1 + own_tiles]),
        pltpu.make_async_copy(right_hbm, right_ref, load_sem.at[2 + own_tiles]),
    ]
    for copy in load_sides:
        copy.start()
    here_lanes = pl.ds(pl.multiple_of(side * BLOCK, BLOCK), BLOCK)
    there_lanes = pl.ds(pl.multiple_of((1 - side) * BLOCK, BLOCK), BLOCK)
    load_train = [
        pltpu.make_async_copy(
            train_hbm.at[pl.ds(j * TILE, TILE), here_lanes], train.at[j], load_sem.at[1 + j]
        )
        for j in range(own_tiles)
    ]
    for copy in load_train:
        copy.start()
    parcels = own_tiles * (TILE // PARCEL)

    def give_train(i):
        return pltpu.make_async_remote_copy(
            src_ref=train_hbm.at[pl.ds(pl.multiple_of(i * PARCEL, PARCEL), PARCEL), there_lanes],
            dst_ref=train.at[
                own_tiles + lax.div(i, TILE // PARCEL),
                pl.ds(pl.multiple_of(lax.rem(i, TILE // PARCEL) * PARCEL, PARCEL), PARCEL),
            ],
            send_sem=train_send.at[i],
            recv_sem=train_recv.at[i],
            device_id={"example": partner},
            device_id_type=MESH,
        )

    row = lax.broadcasted_iota(jnp.int32, (256, 256), 0)
    col = lax.broadcasted_iota(jnp.int32, (256, 256), 1)
    swapper[...] = (lax.bitwise_and(col, 15) * 16 + lax.shift_right_logical(col, 4) == row).astype(
        F32
    ).astype(BF16)
    group_row = lax.bitwise_and(col, 15)
    regroup[...] = (
        lax.bitwise_and(group_row, 1) * (chips * 16)
        + lax.shift_right_logical(group_row, 1) * 16
        + lax.shift_right_logical(col, 4)
        == row
    ).astype(F32).astype(BF16)

    def swap(order):
        return pltpu.make_async_remote_copy(
            src_ref=mine.at[1 - side, order],
            dst_ref=other.at[order],
            send_sem=swap_send.at[order],
            recv_sem=swap_recv.at[order],
            device_id={"example": partner},
            device_id_type=MESH,
        )

    factor = 1.0 / math.sqrt(2 * BLOCK * owners)
    col = lax.broadcasted_iota(jnp.int32, (32, BLOCK), 1)
    row = lax.broadcasted_iota(jnp.int32, (32, BLOCK), 0)
    pick_outer = (lax.shift_right_logical(col, 5) == row).astype(F32)
    pick_inner = (lax.bitwise_and(col, 31) == row).astype(F32)
    for copy in load_sides:
        copy.wait()
    for block, first in ((1 - side, True), (side, False)):
        module = module_ref[param * 2 + block]
        spread_left[...] = lax.dot_general(
            left_ref[module] * factor,
            pick_outer,
            (((0,), (0,)), ((), ())),
            precision=lax.Precision.HIGHEST,
            preferred_element_type=F32,
        )
        spread_right[...] = lax.dot_general(
            right_ref[module],
            pick_inner,
            (((1,), (0,)), ((), ())),
            precision=lax.Precision.HIGHEST,
            preferred_element_type=F32,
        )

        @pl.loop(0, 32)
        def _(b):
            exact = spread_left[pl.ds(b, 1), :] * spread_right[...]
            high = exact.astype(BF16)
            low = (exact - high.astype(F32)).astype(BF16)
            at = pl.ds(pl.multiple_of(b * 32, 32), 32)
            kron_high[at, :] = high
            kron_low[at, :] = low

        if first:
            pl.semaphore_wait(barrier, chips + 3)
            give_train(0).start()
            load_query.wait()
        source = jnp.dot(
            swapper[...], query[:, pl.ds(pl.multiple_of(block * BLOCK, BLOCK), BLOCK)], preferred_element_type=F32
        ).astype(BF16)
        for k in range(BLOCK // TILE):
            cut = slice(k * TILE, (k + 1) * TILE)
            mixed = jnp.dot(source, kron_high[:, cut], preferred_element_type=F32) + jnp.dot(
                source, kron_low[:, cut], preferred_element_type=F32
            )
            mixed = mixed.astype(BF16)
            for part in range(TILE // LANES):
                mine[block, :, k * (TILE // LANES) + part] = mixed[
                    :, part * LANES : (part + 1) * LANES
                ].reshape(GROUPS, 16, LANES)
        if first:

            @pl.loop(0, GROUPS // 2)
            def _(j):
                swap(j).start()
                swap(GROUPS - 1 - j).start()

            @pl.loop(1, parcels)
            def _(i):
                give_train(i).start()

    roots = [lax.div(owner_ref[t], 2) for t in range(turns)]
    sides = [lax.rem(owner_ref[t], 2) for t in range(turns)]
    ahead = [lax.rem(plane - r + ring, ring) for r in roots]
    near = [jnp.where(a <= reach, 0, 1) for a in ahead]
    far_off = [jnp.where(a <= reach, a, ring - a) for a in ahead]
    spare = [reach - f for f in far_off]

    def ring_copy(way, s):
        return pltpu.make_async_remote_copy(
            src_ref=passed.at[way * steps + s],
            dst_ref=landed.at[way * sent + s],
            send_sem=ring_send.at[way * sent + s],
            recv_sem=ring_recv.at[way * sent + s],
            device_id={"example": following if way == 0 else previous},
            device_id_type=MESH,
        )

    def advance(s, first, last):
        j = lax.div(s, PIECES)
        k = lax.rem(s, PIECES)

        @pl.when(jnp.logical_and(k == 0, j < GROUPS // 2))
        def _():
            swap(j).wait_recv()
            swap(GROUPS - 1 - j).wait_recv()

        for way in range(2):
            order = j if way == 0 else GROUPS - 1 - j
            here = mine[side, order, k]
            there = other[order, k]
            if not first:
                ring_copy(way, s - PIECES).wait()
            for t in range(turns):
                value = jnp.where(sides[t] == side, here, there)
                if not first:
                    value = jnp.where(
                        ahead[t] == 0, value, landed[way * sent + s - PIECES, t]
                    )
                passed[way * steps + s, t] = value
            if not last:
                ring_copy(way, s).start()

    def gather(b):
        for u in range(BATCH):
            v = BATCH * b + u
            w = (BATCH // 2) * b + u // 2
            for t in range(turns):
                early = v < 2 * spare[t]
                if u % 2 == 0:
                    way = near[t]
                    lap = jnp.where(early, v, spare[t] + w) + far_off[t]
                else:
                    way = jnp.where(early, near[t], 1 - near[t])
                    lap = jnp.where(early, v + far_off[t], w - spare[t] + ring - far_off[t])
                base = way * steps + lap * PIECES
                for k in range(PIECES):
                    gathered[
                        (u * turns + t) * 16 : (u * turns + t + 1) * 16,
                        k * LANES : (k + 1) * LANES,
                    ] = passed[base + k, t]

    def sort_rows():
        sorted_rows[...] = jnp.dot(
            regroup[...], gathered[...], preferred_element_type=F32
        ).astype(BF16)

    def pair_copy(b, part):
        tiles_of = pl.ds(part * own_tiles, own_tiles)
        return pltpu.make_async_remote_copy(
            src_ref=product.at[b, 1 - core, tiles_of],
            dst_ref=paired.at[b, tiles_of],
            send_sem=pair_send.at[b, part],
            recv_sem=pair_recv.at[b, part],
            device_id={"param": sibling},
            device_id_type=MESH,
        )

    def multiply(b, j):
        product[b, :, j] = lax.dot_general(
            sorted_rows[...], train[j], ACROSS, preferred_element_type=F32
        ).reshape(2, chips * 16, TILE)
        if j % own_tiles == own_tiles - 1:
            pair_copy(b, j // own_tiles).start()

    def sum_copy(b, part, hop):
        tiles_of = pl.ds(part * own_tiles, own_tiles)
        place = lax.rem(chip + hop, chips)
        return pltpu.make_async_remote_copy(
            src_ref=outgoing.at[b, place, tiles_of],
            dst_ref=incoming.at[b, hop, tiles_of],
            send_sem=sum_send.at[b, part, hop],
            recv_sem=sum_recv.at[b, part, hop],
            device_id={"param": place * 2 + core},
            device_id_type=MESH,
        )

    def give(b, part):
        pair_copy(b, part).wait_recv()

        @pl.loop(part * own_tiles, (part + 1) * own_tiles)
        def _(j):
            both = product[b, core, j] + paired[b, j]
            paired[b, j] = both
            outgoing[b, :, j] = both.astype(BF16).reshape(chips, 16, TILE)
            summed[b, j] = paired[b, j, pl.ds(pl.multiple_of(chip * 16, 16), 16), :]

        @pl.loop(1, chips)
        def _(hop):
            sum_copy(b, part, hop).start()

    def cross(b):
        return pltpu.make_async_remote_copy(
            src_ref=summed.at[b, pl.ds(own_tiles, own_tiles)],
            dst_ref=crossed.at[b],
            send_sem=cross_send.at[b],
            recv_sem=cross_recv.at[b],
            device_id={"example": partner},
            device_id_type=MESH,
        )

    def finish(b, part):
        tiles_of = pl.ds(part * own_tiles, own_tiles)

        @pl.loop(1, chips)
        def _(hop):
            sum_copy(b, part, hop).wait_recv()
            summed[b, tiles_of] += incoming[b, hop, tiles_of].astype(F32)

        if part == 1:
            cross(b).start()

    def settle(b):
        cross(b).wait_recv()
        for j in range(own_tiles):
            ordered[j, b * 16 : (b + 1) * 16, :] = summed[b, j] + crossed[b, j]

    start = (reach + 2) * PIECES

    @pl.loop(0, PIECES)
    def _(s):
        advance(s, True, False)

    @pl.loop(PIECES, start)
    def _(s):
        advance(s, False, False)

    for copy in load_train:
        copy.wait()

    def arrived(b, j):
        @pl.when(b == 0)
        def _():
            @pl.loop((j - own_tiles) * (TILE // PARCEL), (j - own_tiles + 1) * (TILE // PARCEL))
            def _(i):
                give_train(i).wait_recv()

    def work(s):
        b = lax.div(s - start, 2 * PIECES)
        k = lax.rem(s - start, 2 * PIECES)

        @pl.when(k == 0)
        def _():
            gather(b)

        @pl.when(k == 1)
        def _():
            sort_rows()
            multiply(b, 0)

        @pl.when(k == 2)
        def _():
            multiply(b, 1)
            multiply(b, 2)

        late = jnp.where(b == 0, 2, 0)

        @pl.when(k == 3 + late)
        def _():
            arrived(b, 3)
            multiply(b, 3)

        @pl.when(k == 4 + late)
        def _():
            arrived(b, 4)
            multiply(b, 4)
            arrived(b, 5)
            multiply(b, 5)

        @pl.when(k == 5 - late)
        def _():
            give(b, 0)

        @pl.when(k == jnp.where(b == 0, 7, 6))
        def _():
            give(b, 1)

        @pl.when(jnp.logical_and(k == 7, b > 0))
        def _():
            finish(b - 1, 1)
            finish(b - 1, 0)

    @pl.loop(start, sent)
    def _(s):
        advance(s, False, False)
        work(s)

    @pl.loop(sent, steps)
    def _(s):
        advance(s, False, True)
        work(s)

    gather(batches - 1)
    sort_rows()
    for j in range(own_tiles, 2 * own_tiles):
        multiply(batches - 1, j)
    multiply(batches - 1, 0)
    give(batches - 1, 1)
    for j in range(1, own_tiles):
        multiply(batches - 1, j)
    give(batches - 1, 0)
    for b in range(2, batches - 1):
        finish(b, 1)
        finish(b, 0)
    for b in range(batches - 2):
        settle(b)
    finish(batches - 1, 1)
    settle(batches - 2)
    finish(batches - 1, 0)

    @pl.loop(0, GROUPS)
    def _(order):
        swap(order).wait_send()

    @pl.loop(0, parcels)
    def _(i):
        give_train(i).wait_send()

    for part in range(2):

        @pl.loop(0, batches)
        def _(b):
            pair_copy(b, part).wait_send()

            @pl.loop(1, chips)
            def _(hop):
                sum_copy(b, part, hop).wait_send()

    settle(batches - 1)

    @pl.loop(0, batches)
    def _(b):
        cross(b).wait_send()

    for t in range(turns):

        @pl.loop(0, GROUPS, unroll=4)
        def _(i):
            a = jnp.where(near[t] == 0, i, GROUPS - 1 - i)
            v = jnp.where(
                a < 2 * spare[t],
                a,
                jnp.where(
                    a < GROUPS // 2 + spare[t],
                    2 * (a - spare[t]),
                    2 * (GROUPS - 1 - a + spare[t]) + 1,
                ),
            )
            for j in range(own_tiles):
                out_ref[i, t : t + 1, j * TILE : (j + 1) * TILE] = ordered[
                    j, pl.ds(v * turns + t, 1), :
                ]


def body(train_grads, query_cache, left_inverse, right_inverse, module_of, owner):
    owners = lax.axis_size("param")
    ring = lax.axis_size("example") // 2
    turns = owner.shape[0]
    rows, coords = train_grads.shape
    queries = query_cache.shape[1]
    own_tiles = rows // TILE
    batches = GROUPS // BATCH
    steps = (GROUPS // 2 + ring // 2) * PIECES
    sent = steps - PIECES
    dma = pltpu.SemaphoreType.DMA
    return pl.pallas_call(
        functools.partial(kernel, ring, turns),
        out_shape=jax.ShapeDtypeStruct((queries // owners, turns, rows), F32),
        in_specs=[
            pl.BlockSpec(memory_space=pl.ANY),
            pl.BlockSpec(memory_space=pl.ANY),
            pl.BlockSpec(memory_space=pl.ANY),
            pl.BlockSpec(memory_space=pl.ANY),
            pl.BlockSpec(memory_space=pltpu.SMEM),
            pl.BlockSpec(memory_space=pltpu.SMEM),
        ],
        out_specs=pl.BlockSpec(memory_space=pltpu.VMEM),
        scratch_shapes=[
            pltpu.VMEM(left_inverse.shape, F32),
            pltpu.VMEM(right_inverse.shape, F32),
            pltpu.VMEM((queries, coords), BF16),
            pltpu.VMEM((2 * own_tiles, TILE, BLOCK), BF16),
            pltpu.VMEM((32, BLOCK), F32),
            pltpu.VMEM((32, BLOCK), F32),
            pltpu.VMEM((BLOCK, BLOCK), BF16),
            pltpu.VMEM((BLOCK, BLOCK), BF16),
            pltpu.VMEM((256, 256), BF16),
            pltpu.VMEM((256, 256), BF16),
            pltpu.VMEM((2, GROUPS, PIECES, 16, LANES), BF16),
            pltpu.VMEM((GROUPS, PIECES, 16, LANES), BF16),
            pltpu.VMEM((2 * sent, turns, 16, LANES), BF16),
            pltpu.VMEM((2 * steps, turns, 16, LANES), BF16),
            pltpu.VMEM((256, BLOCK), BF16),
            pltpu.VMEM((256, BLOCK), BF16),
            pltpu.VMEM((batches, 2, 2 * own_tiles, 8 * owners, TILE), F32),
            pltpu.VMEM((batches, 2 * own_tiles, 8 * owners, TILE), F32),
            pltpu.VMEM((batches, 2 * own_tiles, 16, TILE), F32),
            pltpu.VMEM((batches, own_tiles, 16, TILE), F32),
            pltpu.VMEM((own_tiles, 16 * batches, TILE), F32),
            pltpu.VMEM((batches, owners // 2, 2 * own_tiles, 16, TILE), BF16),
            pltpu.VMEM((batches, owners // 2, 2 * own_tiles, 16, TILE), BF16),
            dma((3 + own_tiles,)),
            dma((GROUPS,)),
            dma((GROUPS,)),
            dma((rows // PARCEL,)),
            dma((rows // PARCEL,)),
            dma((2 * sent,)),
            dma((2 * sent,)),
            dma((batches, 2)),
            dma((batches, 2)),
            dma((batches, 2, owners // 2)),
            dma((batches, 2, owners // 2)),
            dma((batches,)),
            dma((batches,)),
        ],
        compiler_params=pltpu.CompilerParams(
            collective_id=0, has_side_effects=True, vmem_limit_bytes=56 * 1024 * 1024
        ),
    )(train_grads, query_cache, left_inverse, right_inverse, module_of, owner)


def solution(mesh):
    placed = (P("example", "param"), P("example", None, "param"), P(), P(), P(), P())
    return jax.shard_map(
        body, mesh=mesh, in_specs=placed, out_specs=P("param", None, "example"), check_vma=False
    )
```
